32 devices in a mesh: groups: 2 (over x), layer: 16 (over z, y, core).
Axes of the slice: x: 2, y: 2, z: 4, core: 2. Of those that a mesh axis runs over, the one named last changes fastest.
Arguments:
- queries: bfloat16 [128, 32, 1024], P('groups', 'layer'), parts along dimension 0, may hold values from -6 to 6
- inverse_curvature: float32 [32, 1024], P('layer'), may hold values from 0.25 to 4
- store: bfloat16 [64, 32, 1024], P(('groups', 'layer')), parts along dimension 0, may hold values from -6 to 6
- exponents: int32 [64, 32], P(('groups', 'layer')), parts along dimension 0, may hold values from -3 to 1, as said below
Outputs:
- scores: float32 [128, 32], P(('groups', 'layer')), parts along dimension 0
The draws below stay inside these ranges and needn't reach their ends.
There are 2 independent parts, one for each index of `groups`. The reference program is written for one: setup_inputs(seed, part) draws one part's arguments, and reference() takes and returns one part's arrays. A program takes and returns all parts, laid end to end along the dimension named above; an argument that names none is the same for every part. Nothing has to cross between parts.
Inputs may be any that keep to these rules, and one draw needn't show every extreme that they name: `exponents`: exponents of the first half of the matrices lie in -3 to 0, those of the second half in -2 to 1.
All inputs are finite; a program needn't handle non-finite values.
Results may differ from the reference program's by a relative error of at most 0.0029.
Values may be sent and summed in bfloat16 or wider, within the bound.
A program may use at most 64 MiB of HBM per device.

```python
import math
import jax
import jax.numpy as jnp
from jax import lax

FEAT = 1024
MATS = 32
QUERIES = 64
EXAMPLES = 32


def draw_exponents(key, part):
    key = jax.random.fold_in(key, 7)
    base = jax.random.randint(key, (EXAMPLES, MATS), -3, 1)
    base = base.at[0, MATS - 1].set(0)
    base = base.at[0, 0].set(-3)
    rise = 2 * jnp.arange(MATS) // MATS
    return (base + rise[None, :]).astype(jnp.int32)


def spiked(drawn, rng, source, target, parts, factor):
    owner, partner = [(jnp.arange(drawn.shape[position]) // (drawn.shape[position] // parts)).reshape([-1 if axis == position else 1 for axis in range(drawn.ndim)]) for position in (source, target)]
    chosen = jax.random.permutation(rng, parts)[partner]
    strong = (owner == chosen) | (owner == (partner + parts // 2) % parts)
    return jnp.where(strong, factor * drawn, drawn)


def levels(rng, dims, cuts, low, high):
    factor_of, own = 1.0, jax.random.fold_in(rng, 6)
    for axis_at, blocks in cuts:
        steps = jnp.exp(jax.random.uniform(jax.random.fold_in(own, axis_at), (blocks,), jnp.float32, low / len(cuts), high / len(cuts)))
        factor_of = factor_of * jnp.repeat(steps, dims[axis_at] // blocks).reshape([-1 if axis == axis_at else 1 for axis in range(len(dims))])
    return factor_of


def normal_values(own_key, extent, spread, limit, cuts=(), dtype=jnp.bfloat16):
    values = jax.random.normal(own_key, extent, jnp.float32) * spread
    if len(cuts) > 0:
        values = levels(own_key, extent, cuts, -0.22, 0.18) * values
    return jnp.clip(values, min=-limit, max=limit).astype(dtype)


def heavy_noise(stream_key, extent, width, reach, split, heavy, kind=jnp.bfloat16):
    values = width * jax.random.normal(stream_key, extent, jnp.float32)
    if split:
        values = values * levels(stream_key, extent, split, -0.22, 0.18)
    return jnp.clip(spiked(values, jax.random.fold_in(stream_key, 3), *heavy), -reach, reach).astype(kind)


def setup_inputs(seed: int = 0, part: int = 0) -> dict:
    key_list = jax.random.split(jax.random.key(seed), 5)
    part_keys = jax.random.split(jax.random.fold_in(key_list[4], part), 5)
    queries = heavy_noise(part_keys[0], (QUERIES, MATS, FEAT), 1.0, 6.0, ((1, 16),), (1, 0, 16, 2.0))
    inverse_curvature = jnp.clip(jnp.exp(math.log(4.0) - 2.7725887 * jax.random.uniform(key_list[1], (MATS, FEAT), jnp.float32) ** levels(key_list[1], (MATS, FEAT), ((0, 16),), -0.2, 0.2)), 0.25, 4.0)
    store = normal_values(part_keys[2], (EXAMPLES, MATS, FEAT), 1.0, 6.0, ((0, 16),))
    exponents = draw_exponents(jax.random.fold_in(jax.random.fold_in(key_list[4], part), 71), part)
    return {"queries": queries, "inverse_curvature": inverse_curvature, "store": store, "exponents": exponents}


def reference(queries, inverse_curvature, store, exponents):
    weighted = (queries.astype(jnp.float32) * inverse_curvature[None, :, :]).astype(jnp.bfloat16)
    weighted = weighted.reshape(QUERIES, MATS * FEAT)
    factor = jnp.exp2(exponents.astype(jnp.float32))
    decoded = (store.astype(jnp.float32) * factor[:, :, None]).astype(jnp.bfloat16)
    flat = decoded.reshape(EXAMPLES, MATS * FEAT)
    norms = lax.optimization_barrier(jnp.sum(jnp.square(flat.astype(jnp.float32)), axis=1))
    totals = lax.dot_general(weighted, flat, (((1,), (1,)), ((), ())), preferred_element_type=jnp.float32)
    return totals / jnp.sqrt(norms + 1e-06)[None, :]
```

```python
import functools

import jax
import jax.numpy as jnp
from jax import lax
from jax.experimental import pallas as pl
from jax.experimental.pallas import tpu as pltpu
from jax.sharding import PartitionSpec as P

MESH = pl.DeviceIdType.MESH
ROWS = 16
QBLOCK = 64
SBLOCK = 16
MBLOCK = 32


def each(start, stop, body):
    if stop - start <= 16:
        for i in range(start, stop):
            body(i)
    else:
        lax.fori_loop(start, stop, lambda i, c: (body(i), c)[1], 0)


def iota(shape, axis):
    return lax.broadcasted_iota(jnp.int32, shape, axis)


def kernel(
    n,
    q_hbm,
    cur_hbm,
    st_hbm,
    exp_hbm,
    out_ref,
    q_ref,
    cur_ref,
    st_ref,
    exp_ref,
    flat,
    send,
    recv,
    weighted,
    part_send,
    part_recv,
    load_sem,
    send_sem,
    recv_sem,
    psend_sem,
    precv_sem,
):
    me = lax.axis_index("layer")
    ex, mats, feat = st_ref.shape
    count_q, mat_dev, _ = q_ref.shape
    chunks = ROWS // (ex * mat_dev)
    depth = feat // chunks
    sub = ex * chunks
    total = n * ex
    own_q = count_q // n
    lanes = part_send.shape[2]

    loads = [
        pltpu.make_async_copy(src, dst, load_sem.at[i])
        for i, (src, dst) in enumerate(
            [(exp_hbm, exp_ref), (st_hbm, st_ref), (cur_hbm, cur_ref), (q_hbm, q_ref)]
        )
    ]
    for load in loads:
        load.start()

    barrier = pltpu.get_barrier_semaphore()

    def greet(k):
        pl.semaphore_signal(
            barrier, inc=1, device_id={"layer": lax.rem(me + k, n)}, device_id_type=MESH
        )

    each(1, n, greet)

    loads[0].wait()
    loads[1].wait()
    factor_row = jnp.left_shift(1, exp_ref[...] + 3).astype(jnp.float32) * 0.125
    for first in range(0, mats, MBLOCK):
        pick = iota((MBLOCK, mats), 0) + first == iota((MBLOCK, mats), 1)
        for e in range(ex):
            row = jnp.broadcast_to(factor_row[e : e + 1, :], (MBLOCK, mats))
            factor = jnp.sum(jnp.where(pick, row, 0.0), axis=1, keepdims=True)
            grid = st_ref[e, pl.ds(first, MBLOCK), :].astype(jnp.float32) * factor
            for c in range(chunks):
                for t in range(depth // 128):
                    at = c * depth + t * 128
                    flat[t, pl.ds(first * sub + e * chunks + c, MBLOCK, stride=sub), :] = grid[
                        :, at : at + 128
                    ]
    for first in range(0, n, SBLOCK):
        size = min(SBLOCK, n - first)
        for t in range(depth // 128):
            rows = flat[t, pl.ds(first * ROWS, size * ROWS), :].astype(jnp.bfloat16)
            send[pl.ds(first, size), :, pl.ds(t * 128, 128)] = rows.reshape(size, ROWS, 128)

    pl.semaphore_wait(barrier, n - 1)

    def block_copy(peer, slot):
        return pltpu.make_async_remote_copy(
            src_ref=send.at[peer],
            dst_ref=recv.at[slot],
            send_sem=send_sem.at[peer],
            recv_sem=recv_sem.at[slot],
            device_id={"layer": peer},
            device_id_type=MESH,
        )

    def part_copy(peer, slot):
        return pltpu.make_async_remote_copy(
            src_ref=part_send.at[peer],
            dst_ref=part_recv.at[slot],
            send_sem=psend_sem.at[peer],
            recv_sem=precv_sem.at[slot],
            device_id={"layer": peer},
            device_id_type=MESH,
        )

    def peer_of(k):
        return lax.rem(me + k, n)

    each(1, n, lambda k: block_copy(peer_of(k), me).start())
    recv[me] = send[me]

    squares = jnp.zeros((sub, 128), jnp.float32)
    for t in range(depth // 128):
        values = flat[t].reshape(n * mat_dev, sub, 128)
        squares = squares + jnp.sum(values * values, axis=0)
    squares = jnp.sum(squares, axis=1, keepdims=True)
    spot = iota((sub, lanes), 1) == total + me * ex + iota((sub, lanes), 0) // chunks
    norm_row = jnp.sum(jnp.where(spot, squares, 0.0), axis=0, keepdims=True)

    loads[2].wait()
    loads[3].wait()

    def weigh(b):
        rows = pl.ds(b * QBLOCK, QBLOCK)
        grid = q_ref[rows].astype(jnp.float32) * cur_ref[...][None]
        for m in range(mat_dev):
            weighted[m, rows, :] = grid[:, m, :].astype(jnp.bfloat16)

    each(0, count_q // QBLOCK, weigh)

    each(1, n, lambda k: block_copy(peer_of(k), peer_of(k)).wait_recv())

    def score(b):
        rows = pl.ds(b * QBLOCK, QBLOCK)
        result = jnp.broadcast_to(norm_row, (QBLOCK, lanes))
        for first in range(0, n, SBLOCK):
            size = min(SBLOCK, n - first)
            width = size * ROWS
            blocks = recv[pl.ds(first, size)].reshape(width, depth)
            place = lax.rem(iota((QBLOCK, width), 1), ROWS)
            mix = jnp.zeros((QBLOCK, width), jnp.float32)
            for m in range(mat_dev):
                for c in range(chunks):
                    product = lax.dot_general(
                        weighted[m, rows, pl.ds(c * depth, depth)],
                        blocks,
                        (((1,), (1,)), ((), ())),
                        preferred_element_type=jnp.float32,
                    )
                    mine = (place // sub == m) & (lax.rem(place, chunks) == c)
                    mix = jnp.where(mine, product, mix)
            high = mix.astype(jnp.bfloat16)
            rest = mix - high.astype(jnp.float32)
            middle = rest.astype(jnp.bfloat16)
            low = (rest - middle.astype(jnp.float32)).astype(jnp.bfloat16)
            source = iota((width, lanes), 0)
            owner = (first + source // ROWS) * ex + lax.rem(source, sub) // chunks
            fold = jnp.where(owner == iota((width, lanes), 1), 1.0, 0.0).astype(jnp.bfloat16)
            for piece in (low, middle, high):
                result = result + jnp.dot(piece, fold, preferred_element_type=jnp.float32)
        for j in range(QBLOCK // own_q):
            part_send[b * (QBLOCK // own_q) + j] = result[j * own_q : (j + 1) * own_q, :]

    each(0, count_q // QBLOCK, score)

    each(1, n, lambda k: part_copy(peer_of(k), me).start())
    part_recv[me] = part_send[me]
    each(1, n, lambda k: part_copy(peer_of(k), peer_of(k)).wait_recv())
    final = jnp.sum(part_recv[...], axis=0)
    out_ref[...] = final[:, :total] / jnp.sqrt(final[:, total : 2 * total] + 1e-06)

    each(1, n, lambda k: block_copy(peer_of(k), me).wait_send())
    each(1, n, lambda k: part_copy(peer_of(k), me).wait_send())


def solution(mesh):
    n = mesh.shape["layer"]

    def local(queries, inverse_curvature, store, exponents):
        count_q, mat_dev, feat = queries.shape
        ex, mats, _ = store.shape
        chunks = ROWS // (ex * mat_dev)
        depth = feat // chunks
        total = n * ex
        own_q = count_q // n
        lanes = -(-2 * total // 128) * 128
        return pl.pallas_call(
            functools.partial(kernel, n),
            out_shape=jax.ShapeDtypeStruct((own_q, total), jnp.float32),
            in_specs=[pl.BlockSpec(memory_space=pl.ANY)] * 4,
            out_specs=pl.BlockSpec(memory_space=pltpu.VMEM),
            scratch_shapes=[
                pltpu.VMEM(queries.shape, queries.dtype),
                pltpu.VMEM(inverse_curvature.shape, inverse_curvature.dtype),
                pltpu.VMEM(store.shape, store.dtype),
                pltpu.VMEM(exponents.shape, exponents.dtype),
                pltpu.VMEM((depth // 128, n * ROWS, 128), jnp.float32),
                pltpu.VMEM((n, ROWS, depth), jnp.bfloat16),
                pltpu.VMEM((n, ROWS, depth), jnp.bfloat16),
                pltpu.VMEM((mat_dev, count_q, feat), jnp.bfloat16),
                pltpu.VMEM((n, own_q, lanes), jnp.float32),
                pltpu.VMEM((n, own_q, lanes), jnp.float32),
                pltpu.SemaphoreType.DMA((4,)),
                pltpu.SemaphoreType.DMA((n,)),
                pltpu.SemaphoreType.DMA((n,)),
                pltpu.SemaphoreType.DMA((n,)),
                pltpu.SemaphoreType.DMA((n,)),
            ],
            compiler_params=pltpu.CompilerParams(
                collective_id=0, has_side_effects=True, vmem_limit_bytes=32 * 1024 * 1024
            ),
        )(queries, inverse_curvature, store, exponents)

    return jax.shard_map(
        local,
        mesh=mesh,
        in_specs=(
            P("groups", "layer", None),
            P("layer", None),
            P(("groups", "layer"), None, None),
            P(("groups", "layer"), None),
        ),
        out_specs=P(("groups", "layer"), None),
        check_vma=False,
    )
```

```python
import functools

import jax
import jax.numpy as jnp
from jax import lax
from jax.experimental import pallas as pl
from jax.experimental.pallas import tpu as pltpu
from jax.sharding import PartitionSpec as P

MESH = pl.DeviceIdType.MESH
ROWS = 16
QBLOCK = 64
SBLOCK = 16
MBLOCK = 32


def each(start, stop, body):
    if stop - start <= 16:
        for i in range(start, stop):
            body(i)
    else:
        lax.fori_loop(start, stop, lambda i, c: (body(i), c)[1], 0)


def iota(shape, axis):
    return lax.broadcasted_iota(jnp.int32, shape, axis)


def kernel(
    n,
    q_hbm,
    cur_hbm,
    st_hbm,
    exp_hbm,
    out_ref,
    q_ref,
    cur_ref,
    st_ref,
    exp_ref,
    flat,
    send,
    recv,
    weighted,
    part_send,
    part_recv,
    load_sem,
    send_sem,
    recv_sem,
    psend_sem,
    precv_sem,
):
    me = lax.axis_index("layer")
    ex, mats, feat = st_ref.shape
    count_q, mat_dev, _ = q_ref.shape
    chunks = ROWS // (ex * mat_dev)
    depth = feat // chunks
    sub = ex * chunks
    total = n * ex
    own_q = count_q // n
    lanes = part_send.shape[2]

    loads = [
        pltpu.make_async_copy(src, dst, load_sem.at[i])
        for i, (src, dst) in enumerate(
            [(exp_hbm, exp_ref), (st_hbm, st_ref), (cur_hbm, cur_ref), (q_hbm, q_ref)]
        )
    ]
    for load in loads:
        load.start()

    def peer_of(k):
        if n & (n - 1):
            return lax.rem(me + k, n)
        step = n - k
        peer = me
        bit = 1
        while bit < n:
            flip = step // bit % 2
            peer = peer + flip * bit * (1 - 2 * lax.rem(me // bit, 2))
            bit *= 2
        return peer

    barrier = pltpu.get_barrier_semaphore()

    def greet(k):
        pl.semaphore_signal(
            barrier, inc=1, device_id={"layer": peer_of(k)}, device_id_type=MESH
        )

    each(1, n, greet)

    loads[0].wait()
    loads[1].wait()
    factor_row = jnp.left_shift(1, exp_ref[...] + 3).astype(jnp.float32) * 0.125
    for first in range(0, mats, MBLOCK):
        pick = iota((MBLOCK, mats), 0) + first == iota((MBLOCK, mats), 1)
        for e in range(ex):
            row = jnp.broadcast_to(factor_row[e : e + 1, :], (MBLOCK, mats))
            factor = jnp.sum(jnp.where(pick, row, 0.0), axis=1, keepdims=True)
            grid = st_ref[e, pl.ds(first, MBLOCK), :].astype(jnp.float32) * factor
            for c in range(chunks):
                for t in range(depth // 128):
                    at = c * depth + t * 128
                    flat[t, pl.ds(first * sub + e * chunks + c, MBLOCK, stride=sub), :] = grid[
                        :, at : at + 128
                    ]
    for first in range(0, n, SBLOCK):
        size = min(SBLOCK, n - first)
        for t in range(depth // 128):
            rows = flat[t, pl.ds(first * ROWS, size * ROWS), :].astype(jnp.bfloat16)
            send[pl.ds(first, size), :, pl.ds(t * 128, 128)] = rows.reshape(size, ROWS, 128)

    pl.semaphore_wait(barrier, n - 1)

    def block_copy(peer, slot):
        return pltpu.make_async_remote_copy(
            src_ref=send.at[peer],
            dst_ref=recv.at[slot],
            send_sem=send_sem.at[peer],
            recv_sem=recv_sem.at[slot],
            device_id={"layer": peer},
            device_id_type=MESH,
        )

    def part_copy(peer, slot):
        return pltpu.make_async_remote_copy(
            src_ref=part_send.at[peer],
            dst_ref=part_recv.at[slot],
            send_sem=psend_sem.at[peer],
            recv_sem=precv_sem.at[slot],
            device_id={"layer": peer},
            device_id_type=MESH,
        )

    each(1, n, lambda k: block_copy(peer_of(k), me).start())
    recv[me] = send[me]

    squares = jnp.zeros((sub, 128), jnp.float32)
    for t in range(depth // 128):
        values = flat[t].reshape(n * mat_dev, sub, 128)
        squares = squares + jnp.sum(values * values, axis=0)
    squares = jnp.sum(squares, axis=1, keepdims=True)
    spot = iota((sub, lanes), 1) == total + me * ex + iota((sub, lanes), 0) // chunks
    norm_row = jnp.sum(jnp.where(spot, squares, 0.0), axis=0, keepdims=True)

    loads[2].wait()
    loads[3].wait()

    def weigh(b):
        rows = pl.ds(b * QBLOCK, QBLOCK)
        grid = q_ref[rows].astype(jnp.float32) * cur_ref[...][None]
        for m in range(mat_dev):
            weighted[m, rows, :] = grid[:, m, :].astype(jnp.bfloat16)

    each(0, count_q // QBLOCK, weigh)

    each(1, n, lambda k: block_copy(peer_of(k), peer_of(k)).wait_recv())

    def score(b):
        rows = pl.ds(b * QBLOCK, QBLOCK)
        result = jnp.broadcast_to(norm_row, (QBLOCK, lanes))
        for first in range(0, n, SBLOCK):
            size = min(SBLOCK, n - first)
            width = size * ROWS
            blocks = recv[pl.ds(first, size)].reshape(width, depth)
            place = lax.rem(iota((QBLOCK, width), 1), ROWS)
            mix = jnp.zeros((QBLOCK, width), jnp.float32)
            for m in range(mat_dev):
                for c in range(chunks):
                    product = lax.dot_general(
                        weighted[m, rows, pl.ds(c * depth, depth)],
                        blocks,
                        (((1,), (1,)), ((), ())),
                        preferred_element_type=jnp.float32,
                    )
                    mine = (place // sub == m) & (lax.rem(place, chunks) == c)
                    mix = jnp.where(mine, product, mix)
            high = mix.astype(jnp.bfloat16)
            rest = mix - high.astype(jnp.float32)
            middle = rest.astype(jnp.bfloat16)
            low = (rest - middle.astype(jnp.float32)).astype(jnp.bfloat16)
            source = iota((width, lanes), 0)
            owner = (first + source // ROWS) * ex + lax.rem(source, sub) // chunks
            fold = jnp.where(owner == iota((width, lanes), 1), 1.0, 0.0).astype(jnp.bfloat16)
            for piece in (low, middle, high):
                result = result + jnp.dot(piece, fold, preferred_element_type=jnp.float32)
        for j in range(QBLOCK // own_q):
            part_send[b * (QBLOCK // own_q) + j] = result[j * own_q : (j + 1) * own_q, :]

    each(0, count_q // QBLOCK, score)

    each(1, n, lambda k: part_copy(peer_of(k), me).start())
    part_recv[me] = part_send[me]
    each(1, n, lambda k: part_copy(peer_of(k), peer_of(k)).wait_recv())
    final = jnp.sum(part_recv[...], axis=0)
    out_ref[...] = final[:, :total] / jnp.sqrt(final[:, total : 2 * total] + 1e-06)

    each(1, n, lambda k: block_copy(peer_of(k), me).wait_send())
    each(1, n, lambda k: part_copy(peer_of(k), me).wait_send())


def solution(mesh):
    n = mesh.shape["layer"]

    def local(queries, inverse_curvature, store, exponents):
        count_q, mat_dev, feat = queries.shape
        ex, mats, _ = store.shape
        chunks = ROWS // (ex * mat_dev)
        depth = feat // chunks
        total = n * ex
        own_q = count_q // n
        lanes = -(-2 * total // 128) * 128
        return pl.pallas_call(
            functools.partial(kernel, n),
            out_shape=pltpu.VMEM((own_q, total), jnp.float32),
            in_specs=[pl.BlockSpec(memory_space=pl.ANY)] * 4,
            out_specs=pl.BlockSpec(memory_space=pltpu.VMEM),
            scratch_shapes=[
                pltpu.VMEM(queries.shape, queries.dtype),
                pltpu.VMEM(inverse_curvature.shape, inverse_curvature.dtype),
                pltpu.VMEM(store.shape, store.dtype),
                pltpu.VMEM(exponents.shape, exponents.dtype),
                pltpu.VMEM((depth // 128, n * ROWS, 128), jnp.float32),
                pltpu.VMEM((n, ROWS, depth), jnp.bfloat16),
                pltpu.VMEM((n, ROWS, depth), jnp.bfloat16),
                pltpu.VMEM((mat_dev, count_q, feat), jnp.bfloat16),
                pltpu.VMEM((n, own_q, lanes), jnp.float32),
                pltpu.VMEM((n, own_q, lanes), jnp.float32),
                pltpu.SemaphoreType.DMA((4,)),
                pltpu.SemaphoreType.DMA((n,)),
                pltpu.SemaphoreType.DMA((n,)),
                pltpu.SemaphoreType.DMA((n,)),
                pltpu.SemaphoreType.DMA((n,)),
            ],
            compiler_params=pltpu.CompilerParams(
                collective_id=0, has_side_effects=True
            ),
        )(queries, inverse_curvature, store, exponents)

    return jax.shard_map(
        local,
        mesh=mesh,
        in_specs=(
            P("groups", "layer", None),
            P("layer", None),
            P(("groups", "layer"), None, None),
            P(("groups", "layer"), None),
        ),
        out_specs=P(("groups", "layer"), None),
        check_vma=False,
    )
```

```python
import functools

import jax
import jax.numpy as jnp
from jax import lax
from jax.experimental import pallas as pl
from jax.experimental.pallas import tpu as pltpu
from jax.sharding import PartitionSpec as P

MESH = pl.DeviceIdType.MESH
ROWS = 16
QBLOCK = 64
SBLOCK = 16
MBLOCK = 32


def each(start, stop, body):
    if stop - start <= 16:
        for i in range(start, stop):
            body(i)
    else:
        lax.fori_loop(start, stop, lambda i, c: (body(i), c)[1], 0)


def iota(shape, axis):
    return lax.broadcasted_iota(jnp.int32, shape, axis)


def kernel(
    n,
    q_hbm,
    cur_hbm,
    st_hbm,
    exp_hbm,
    out_ref,
    q_ref,
    cur_ref,
    st_ref,
    exp_ref,
    flat,
    send,
    recv,
    weighted,
    fold,
    part_send,
    part_recv,
    load_sem,
    send_sem,
    recv_sem,
    psend_sem,
    precv_sem,
):
    me = lax.axis_index("layer")
    ex, mats, feat = st_ref.shape
    count_q, mat_dev, _ = q_ref.shape
    chunks = ROWS // (ex * mat_dev)
    depth = feat // chunks
    sub = ex * chunks
    total = n * ex
    own_q = count_q // n
    lanes = part_send.shape[2]

    def peer_of(k):
        if n & (n - 1):
            return lax.rem(me + k, n)
        step = n - k
        peer = me
        bit = 1
        while bit < n:
            flip = step // bit % 2
            peer = peer + flip * bit * (1 - 2 * lax.rem(me // bit, 2))
            bit *= 2
        return peer

    barrier = pltpu.get_barrier_semaphore()

    def greet(k):
        pl.semaphore_signal(
            barrier, inc=1, device_id={"layer": peer_of(k)}, device_id_type=MESH
        )

    each(1, n, greet)

    loads = [
        pltpu.make_async_copy(src, dst, load_sem.at[i])
        for i, (src, dst) in enumerate(
            [(exp_hbm, exp_ref), (st_hbm, st_ref), (cur_hbm, cur_ref), (q_hbm, q_ref)]
        )
    ]
    for load in loads:
        load.start()

    loads[0].wait()
    loads[1].wait()
    factor_row = jnp.left_shift(1, exp_ref[...] + 3).astype(jnp.float32) * 0.125
    for first in range(0, mats, MBLOCK):
        pick = iota((MBLOCK, mats), 0) + first == iota((MBLOCK, mats), 1)
        for e in range(ex):
            row = jnp.broadcast_to(factor_row[e : e + 1, :], (MBLOCK, mats))
            factor = jnp.sum(jnp.where(pick, row, 0.0), axis=1, keepdims=True)
            grid = st_ref[e, pl.ds(first, MBLOCK), :].astype(jnp.float32) * factor
            for c in range(chunks):
                for t in range(depth // 128):
                    at = c * depth + t * 128
                    flat[t, pl.ds(first * sub + e * chunks + c, MBLOCK, stride=sub), :] = grid[
                        :, at : at + 128
                    ]
    for first in range(0, n, SBLOCK):
        size = min(SBLOCK, n - first)
        for t in range(depth // 128):
            rows = flat[t, pl.ds(first * ROWS, size * ROWS), :].astype(jnp.bfloat16)
            send[pl.ds(first, size), :, pl.ds(t * 128, 128)] = rows.reshape(size, ROWS, 128)

    pl.semaphore_wait(barrier, n - 1)

    def block_copy(peer, slot):
        return pltpu.make_async_remote_copy(
            src_ref=send.at[peer],
            dst_ref=recv.at[slot],
            send_sem=send_sem.at[peer],
            recv_sem=recv_sem.at[slot],
            device_id={"layer": peer},
            device_id_type=MESH,
        )

    def part_copy(peer, slot):
        return pltpu.make_async_remote_copy(
            src_ref=part_send.at[peer],
            dst_ref=part_recv.at[slot],
            send_sem=psend_sem.at[peer],
            recv_sem=precv_sem.at[slot],
            device_id={"layer": peer},
            device_id_type=MESH,
        )

    each(1, n, lambda k: block_copy(peer_of(k), me).start())
    recv[me] = send[me]

    squares = jnp.zeros((sub, 128), jnp.float32)
    for t in range(depth // 128):
        values = flat[t].reshape(n * mat_dev, sub, 128)
        squares = squares + jnp.sum(values * values, axis=0)
    squares = jnp.sum(squares, axis=1, keepdims=True)
    spot = iota((sub, lanes), 1) == total + me * ex + iota((sub, lanes), 0) // chunks
    norm_row = jnp.sum(jnp.where(spot, squares, 0.0), axis=0, keepdims=True)

    loads[2].wait()
    loads[3].wait()

    def weigh(b):
        rows = pl.ds(b * QBLOCK, QBLOCK)
        grid = q_ref[rows].astype(jnp.float32) * cur_ref[...][None]
        for m in range(mat_dev):
            plane = grid[:, m, :].astype(jnp.bfloat16)
            for c in range(chunks):
                at = pl.ds((m * chunks + c) * QBLOCK, QBLOCK)
                weighted[b, at, :] = plane[:, c * depth : (c + 1) * depth]

    each(0, count_q // QBLOCK, weigh)

    for first in range(0, n, SBLOCK):
        size = min(SBLOCK, n - first)
        source = iota((size * ROWS, lanes), 0)
        owner = (first + source // ROWS) * ex + lax.rem(source, sub) // chunks
        ones = jnp.where(owner == iota((size * ROWS, lanes), 1), 1.0, 0.0)
        fold[pl.ds(first * ROWS, size * ROWS), :] = ones.astype(jnp.bfloat16)

    each(1, n, lambda k: block_copy(peer_of(k), peer_of(k)).wait_recv())

    def score(b):
        rows = pl.ds(b * QBLOCK, QBLOCK)
        result = jnp.broadcast_to(norm_row, (QBLOCK, lanes))
        for first in range(0, n, SBLOCK):
            size = min(SBLOCK, n - first)
            width = size * ROWS
            blocks = recv[pl.ds(first, size)].reshape(width, depth)
            products = lax.dot_general(
                weighted[b], blocks, (((1,), (1,)), ((), ())), preferred_element_type=jnp.float32
            )
            kept = [products[i * QBLOCK : (i + 1) * QBLOCK] for i in range(mat_dev * chunks)]
            place = iota((QBLOCK, width), 1)
            bit = 1
            while len(kept) > 1:
                odd = jnp.bitwise_and(place, bit) != 0
                kept = [jnp.where(odd, kept[i + 1], kept[i]) for i in range(0, len(kept), 2)]
                bit *= 2
                if bit == chunks:
                    bit = sub
            mix = kept[0]
            high = mix.astype(jnp.bfloat16)
            rest = mix - high.astype(jnp.float32)
            low = rest.astype(jnp.bfloat16)
            pieces = jnp.dot(
                jnp.concatenate([high, low], axis=0),
                fold[pl.ds(first * ROWS, width), :],
                preferred_element_type=jnp.float32,
            )
            result = result + (pieces[QBLOCK:] + pieces[:QBLOCK])
        for j in range(QBLOCK // own_q):
            part_send[b * (QBLOCK // own_q) + j] = result[j * own_q : (j + 1) * own_q, :]

    each(0, count_q // QBLOCK, score)

    each(1, n, lambda k: part_copy(peer_of(k), me).start())
    part_recv[me] = part_send[me]
    each(1, n, lambda k: part_copy(peer_of(k), peer_of(k)).wait_recv())
    final = jnp.sum(part_recv[...], axis=0)
    out_ref[...] = final[:, :total] / jnp.sqrt(final[:, total : 2 * total] + 1e-06)

    each(1, n, lambda k: block_copy(peer_of(k), me).wait_send())
    each(1, n, lambda k: part_copy(peer_of(k), me).wait_send())


def solution(mesh):
    n = mesh.shape["layer"]

    def local(queries, inverse_curvature, store, exponents):
        count_q, mat_dev, feat = queries.shape
        ex, mats, _ = store.shape
        chunks = ROWS // (ex * mat_dev)
        depth = feat // chunks
        total = n * ex
        own_q = count_q // n
        lanes = -(-2 * total // 128) * 128
        return pl.pallas_call(
            functools.partial(kernel, n),
            out_shape=pltpu.VMEM((own_q, total), jnp.float32),
            in_specs=[pl.BlockSpec(memory_space=pl.ANY)] * 4,
            out_specs=pl.BlockSpec(memory_space=pltpu.VMEM),
            scratch_shapes=[
                pltpu.VMEM(queries.shape, queries.dtype),
                pltpu.VMEM(inverse_curvature.shape, inverse_curvature.dtype),
                pltpu.VMEM(store.shape, store.dtype),
                pltpu.VMEM(exponents.shape, exponents.dtype),
                pltpu.VMEM((depth // 128, n * ROWS, 128), jnp.float32),
                pltpu.VMEM((n, ROWS, depth), jnp.bfloat16),
                pltpu.VMEM((n, ROWS, depth), jnp.bfloat16),
                pltpu.VMEM((count_q // QBLOCK, QBLOCK * mat_dev * chunks, depth), jnp.bfloat16),
                pltpu.VMEM((n * ROWS, lanes), jnp.bfloat16),
                pltpu.VMEM((n, own_q, lanes), jnp.float32),
                pltpu.VMEM((n, own_q, lanes), jnp.float32),
                pltpu.SemaphoreType.DMA((4,)),
                pltpu.SemaphoreType.DMA((n,)),
                pltpu.SemaphoreType.DMA((n,)),
                pltpu.SemaphoreType.DMA((n,)),
                pltpu.SemaphoreType.DMA((n,)),
            ],
            compiler_params=pltpu.CompilerParams(
                collective_id=0, has_side_effects=True
            ),
        )(queries, inverse_curvature, store, exponents)

    return jax.shard_map(
        local,
        mesh=mesh,
        in_specs=(
            P("groups", "layer", None),
            P("layer", None),
            P(("groups", "layer"), None, None),
            P(("groups", "layer"), None),
        ),
        out_specs=P(("groups", "layer"), None),
        check_vma=False,
    )
```

```python
import functools

import jax
import jax.numpy as jnp
from jax import lax
from jax.experimental import pallas as pl
from jax.experimental.pallas import tpu as pltpu
from jax.sharding import PartitionSpec as P

MESH = pl.DeviceIdType.MESH
ROWS = 16
QBLOCK = 64
SBLOCK = 16
MBLOCK = 32


def each(start, stop, body):
    if stop - start <= 16:
        for i in range(start, stop):
            body(i)
    else:
        lax.fori_loop(start, stop, lambda i, c: (body(i), c)[1], 0)


def iota(shape, axis):
    return lax.broadcasted_iota(jnp.int32, shape, axis)


def kernel(
    n,
    q_hbm,
    cur_hbm,
    st_hbm,
    exp_hbm,
    out_ref,
    q_ref,
    cur_ref,
    st_ref,
    exp_ref,
    flat,
    send,
    recv,
    weighted,
    fold,
    part_send,
    part_recv,
    load_sem,
    send_sem,
    recv_sem,
    psend_sem,
    precv_sem,
):
    me = lax.axis_index("layer")
    ex, mats, feat = st_ref.shape
    count_q, mat_dev, _ = q_ref.shape
    chunks = ROWS // (ex * mat_dev)
    depth = feat // chunks
    sub = ex * chunks
    total = n * ex
    own_q = count_q // n
    lanes = part_send.shape[2]

    def peer_of(k):
        if n & (n - 1):
            return lax.rem(me + k, n)
        step = n - k
        peer = me
        bit = 1
        while bit < n:
            flip = step // bit % 2
            peer = peer + flip * bit * (1 - 2 * lax.rem(me // bit, 2))
            bit *= 2
        return peer

    barrier = pltpu.get_barrier_semaphore()

    def greet(k):
        pl.semaphore_signal(
            barrier, inc=1, device_id={"layer": peer_of(k)}, device_id_type=MESH
        )

    each(1, n, greet)

    loads = [
        pltpu.make_async_copy(src, dst, load_sem.at[i])
        for i, (src, dst) in enumerate(
            [(exp_hbm, exp_ref), (st_hbm, st_ref), (cur_hbm, cur_ref), (q_hbm, q_ref)]
        )
    ]
    for load in loads:
        load.start()

    loads[0].wait()
    loads[1].wait()
    factor_row = jnp.left_shift(1, exp_ref[...] + 3).astype(jnp.float32) * 0.125
    for first in range(0, mats, MBLOCK):
        pick = iota((MBLOCK, mats), 0) + first == iota((MBLOCK, mats), 1)
        for e in range(ex):
            row = jnp.broadcast_to(factor_row[e : e + 1, :], (MBLOCK, mats))
            factor = jnp.sum(jnp.where(pick, row, 0.0), axis=1, keepdims=True)
            grid = st_ref[e, pl.ds(first, MBLOCK), :].astype(jnp.float32) * factor
            for c in range(chunks):
                for t in range(depth // 128):
                    at = c * depth + t * 128
                    flat[t, pl.ds(first * sub + e * chunks + c, MBLOCK, stride=sub), :] = grid[
                        :, at : at + 128
                    ]
    for first in range(0, n, SBLOCK):
        size = min(SBLOCK, n - first)
        for t in range(depth // 128):
            rows = flat[t, pl.ds(first * ROWS, size * ROWS), :].astype(jnp.bfloat16)
            send[pl.ds(first, size), :, pl.ds(t * 128, 128)] = rows.reshape(size, ROWS, 128)

    pl.semaphore_wait(barrier, n - 1)

    def block_copy(peer, slot):
        return pltpu.make_async_remote_copy(
            src_ref=send.at[peer],
            dst_ref=recv.at[slot],
            send_sem=send_sem,
            recv_sem=recv_sem,
            device_id={"layer": peer},
            device_id_type=MESH,
        )

    def part_copy(peer, slot):
        return pltpu.make_async_remote_copy(
            src_ref=part_send.at[peer],
            dst_ref=part_recv.at[slot],
            send_sem=psend_sem,
            recv_sem=precv_sem,
            device_id={"layer": peer},
            device_id_type=MESH,
        )

    def all_of(src, dst, sent, received):
        most = pl.ds(0, n - 1)
        return pltpu.make_async_remote_copy(
            src_ref=src.at[most],
            dst_ref=dst.at[most],
            send_sem=sent,
            recv_sem=received,
            device_id={"layer": peer_of(1)},
            device_id_type=MESH,
        )

    each(1, n, lambda k: block_copy(peer_of(k), me).start())
    recv[me] = send[me]

    squares = jnp.zeros((sub, 128), jnp.float32)
    for t in range(depth // 128):
        values = flat[t].reshape(n * mat_dev, sub, 128)
        squares = squares + jnp.sum(values * values, axis=0)
    squares = jnp.sum(squares, axis=1, keepdims=True)
    spot = iota((sub, lanes), 1) == total + me * ex + iota((sub, lanes), 0) // chunks
    norm_row = jnp.sum(jnp.where(spot, squares, 0.0), axis=0, keepdims=True)

    loads[2].wait()
    loads[3].wait()

    def weigh(b):
        rows = pl.ds(b * QBLOCK, QBLOCK)
        grid = q_ref[rows].astype(jnp.float32) * cur_ref[...][None]
        for m in range(mat_dev):
            plane = grid[:, m, :].astype(jnp.bfloat16)
            for c in range(chunks):
                at = pl.ds((m * chunks + c) * QBLOCK, QBLOCK)
                weighted[b, at, :] = plane[:, c * depth : (c + 1) * depth]

    each(0, count_q // QBLOCK, weigh)

    for first in range(0, n, SBLOCK):
        size = min(SBLOCK, n - first)
        source = iota((size * ROWS, lanes), 0)
        owner = (first + source // ROWS) * ex + lax.rem(source, sub) // chunks
        ones = jnp.where(owner == iota((size * ROWS, lanes), 1), 1.0, 0.0)
        fold[pl.ds(first * ROWS, size * ROWS), :] = ones.astype(jnp.bfloat16)

    all_of(send, recv, send_sem, recv_sem).wait_recv()

    def score(b):
        rows = pl.ds(b * QBLOCK, QBLOCK)
        result = jnp.broadcast_to(norm_row, (QBLOCK, lanes))
        for first in range(0, n, SBLOCK):
            size = min(SBLOCK, n - first)
            width = size * ROWS
            blocks = recv[pl.ds(first, size)].reshape(width, depth)
            products = lax.dot_general(
                weighted[b], blocks, (((1,), (1,)), ((), ())), preferred_element_type=jnp.float32
            )
            kept = [products[i * QBLOCK : (i + 1) * QBLOCK] for i in range(mat_dev * chunks)]
            place = iota((QBLOCK, width), 1)
            bit = 1
            while len(kept) > 1:
                odd = jnp.bitwise_and(place, bit) != 0
                kept = [jnp.where(odd, kept[i + 1], kept[i]) for i in range(0, len(kept), 2)]
                bit *= 2
                if bit == chunks:
                    bit = sub
            mix = kept[0]
            high = mix.astype(jnp.bfloat16)
            rest = mix - high.astype(jnp.float32)
            low = rest.astype(jnp.bfloat16)
            pieces = jnp.dot(
                jnp.concatenate([high, low], axis=0),
                fold[pl.ds(first * ROWS, width), :],
                preferred_element_type=jnp.float32,
            )
            result = result + (pieces[QBLOCK:] + pieces[:QBLOCK])
        for j in range(QBLOCK // own_q):
            part_send[b * (QBLOCK // own_q) + j] = result[j * own_q : (j + 1) * own_q, :]

    each(0, count_q // QBLOCK, score)

    each(1, n, lambda k: part_copy(peer_of(k), me).start())
    part_recv[me] = part_send[me]
    all_of(part_send, part_recv, psend_sem, precv_sem).wait_recv()
    final = jnp.sum(part_recv[...], axis=0)
    out_ref[...] = final[:, :total] / jnp.sqrt(final[:, total : 2 * total] + 1e-06)

    all_of(send, recv, send_sem, recv_sem).wait_send()
    all_of(part_send, part_recv, psend_sem, precv_sem).wait_send()


def solution(mesh):
    n = mesh.shape["layer"]

    def local(queries, inverse_curvature, store, exponents):
        count_q, mat_dev, feat = queries.shape
        ex, mats, _ = store.shape
        chunks = ROWS // (ex * mat_dev)
        depth = feat // chunks
        total = n * ex
        own_q = count_q // n
        lanes = -(-2 * total // 128) * 128
        return pl.pallas_call(
            functools.partial(kernel, n),
            out_shape=pltpu.VMEM((own_q, total), jnp.float32),
            in_specs=[pl.BlockSpec(memory_space=pl.ANY)] * 4,
            out_specs=pl.BlockSpec(memory_space=pltpu.VMEM),
            scratch_shapes=[
                pltpu.VMEM(queries.shape, queries.dtype),
                pltpu.VMEM(inverse_curvature.shape, inverse_curvature.dtype),
                pltpu.VMEM(store.shape, store.dtype),
                pltpu.VMEM(exponents.shape, exponents.dtype),
                pltpu.VMEM((depth // 128, n * ROWS, 128), jnp.float32),
                pltpu.VMEM((n, ROWS, depth), jnp.bfloat16),
                pltpu.VMEM((n, ROWS, depth), jnp.bfloat16),
                pltpu.VMEM((count_q // QBLOCK, QBLOCK * mat_dev * chunks, depth), jnp.bfloat16),
                pltpu.VMEM((n * ROWS, lanes), jnp.bfloat16),
                pltpu.VMEM((n, own_q, lanes), jnp.float32),
                pltpu.VMEM((n, own_q, lanes), jnp.float32),
                pltpu.SemaphoreType.DMA((4,)),
                pltpu.SemaphoreType.DMA(()),
                pltpu.SemaphoreType.DMA(()),
                pltpu.SemaphoreType.DMA(()),
                pltpu.SemaphoreType.DMA(()),
            ],
            compiler_params=pltpu.CompilerParams(
                collective_id=0, has_side_effects=True
            ),
        )(queries, inverse_curvature, store, exponents)

    return jax.shard_map(
        local,
        mesh=mesh,
        in_specs=(
            P("groups", "layer", None),
            P("layer", None),
            P(("groups", "layer"), None, None),
            P(("groups", "layer"), None),
        ),
        out_specs=P(("groups", "layer"), None),
        check_vma=False,
    )
```
